256 devices in a mesh: group: 16 (over x_hi, y, core), fsdp: 16 (over x_lo, z).
Axes of the slice: x: 4 (x_hi: 2, x_lo: 2; x = x_hi * 2 + x_lo), y: 4, z: 8, core: 2. Of those that a mesh axis runs over, the one named last changes fastest.
Arguments:
- activations: bfloat16 [65536, 384], P(('group', 'fsdp')), may hold values from -6 to 6
- cotangent: bfloat16 [65536, 14336], P(('group', 'fsdp')), may hold values from -0.09375 to 0.09375
- params: float32 [16, 384, 14336], P('group', 'fsdp'), may hold values from -6 to 6
- moment: float32 [16, 384, 14336], P('group', 'fsdp'), may hold values from -3 to 3
- step_index: int32 [], replicated, may hold values from 0 to 999
Outputs:
- new_params: float32 [16, 384, 14336], P('group', 'fsdp')
- new_moment: float32 [16, 384, 14336], P('group', 'fsdp')
The draws below stay inside these ranges and needn't reach their ends.
All inputs are finite; a program needn't handle non-finite values.
Results may differ from the reference program's by a relative error of at most 0.0009.
Values may be sent and summed in bfloat16 or wider, within the bound.
A program may use at most 256 MiB of HBM per device.

```python
import jax
import jax.numpy as jnp
from jax import lax

HID = 14336
TOK_DEV = 256
WROWS = 384
REPLICAS = 16
TOKENS = 65536
N_GROUP = 16
N_FSDP = 16


def steps_of(key, dims, cuts, least, high):
    level, own = 1.0, jax.random.fold_in(key, 6)
    for axis_at, blocks in cuts:
        heights = jnp.exp(jax.random.uniform(jax.random.fold_in(own, axis_at), (blocks,), jnp.float32, least / len(cuts), high / len(cuts)))
        level = level * jnp.repeat(heights, dims[axis_at] // blocks).reshape([-1 if axis == axis_at else 1 for axis in range(len(dims))])
    return level


def scatter_about(key, extent, width, reach, shards=(), held_as=jnp.bfloat16):
    values = width * jax.random.normal(key, extent, jnp.float32)
    if shards:
        values = values * steps_of(key, extent, shards, -0.22, 0.18)
    return jnp.clip(values, -reach, reach).astype(held_as)


def setup_inputs(seed: int = 0) -> dict:
    key_list = jax.random.split(jax.random.key(seed), 6)
    activations = scatter_about(key_list[0], (TOKENS, WROWS), 1.0, 6.0, ((0, 256),))
    cotangent = scatter_about(key_list[1], (TOKENS, HID), (1.0 / (TOK_DEV * N_FSDP) ** 0.5), 0.09375, ((0, 256),))
    params = scatter_about(key_list[2], (REPLICAS, WROWS, HID), 1.0, 6.0, ((0, 16), (1, 16)), jnp.float32)
    moment = scatter_about(key_list[3], (REPLICAS, WROWS, HID), 0.5, 3.0, ((0, 16), (1, 16)), jnp.float32)
    step_index = jax.random.randint(key_list[4], (), 0, 1000).astype(jnp.int32)
    return dict(activations=activations, cotangent=cotangent, params=params, moment=moment, step_index=step_index)


rate_step = 0.1
momentum_coef = 0.9

def group_grad(inputs):
    group_acts, group_cot = inputs
    return lax.dot_general(group_acts, group_cot, (((0,), (0,)), ((), ())), preferred_element_type=jnp.float32)

def reference(activations, cotangent, params, moment, step_index):
    group_acts = activations.reshape(N_GROUP, TOK_DEV * N_FSDP, WROWS)
    group_cot = cotangent.reshape(N_GROUP, TOK_DEV * N_FSDP, HID)
    grad = lax.map(group_grad, (group_acts, group_cot))
    new_moment = momentum_coef * moment + grad
    half_step = params - rate_step * (grad + momentum_coef * new_moment)
    bit_count = N_GROUP.bit_length() - 1
    exponent = (step_index % bit_count).astype(jnp.int32)
    distance = jnp.left_shift(jnp.int32(1), exponent)
    partner = jnp.bitwise_xor(jnp.arange(N_GROUP, dtype=jnp.int32), distance)
    new_params = 0.5 * (half_step + half_step[partner])
    return (new_params, new_moment)
```

```python
from functools import partial

import jax
import jax.numpy as jnp
from jax import lax
from jax.experimental import pallas as pl
from jax.experimental.pallas import tpu as pltpu
from jax.sharding import PartitionSpec as P

RATE = 0.1
MOMENTUM = 0.9

HID = 14336
TOK = 256
WROWS = 384
ROWS = 24
NZ_RING = 8
C = 512

CODE_LOW = 30.0
CODE_HIGH = 11.2
CODE_STEPS = 32766.0 / (CODE_LOW + CODE_HIGH)
CODE_TINY = 2.0**-30

MESH = pl.DeviceIdType.MESH
PAIR_SLOTS = (2, 3, 5, 6, 8, 9, 11, 12, 14, 15)
UNITS = 18
HOP_LAG = 1
FIN_LAG = 1
MATE_LAG = 1
AHEAD = 2


def encode(v):
    size = jnp.maximum(jnp.abs(v), CODE_TINY)
    level = jnp.log2(size) * CODE_STEPS + (CODE_LOW * CODE_STEPS + 0.5)
    return jnp.where(v < 0.0, -level, level).astype(jnp.int32).astype(jnp.int16)


def decode(q):
    level = q.astype(jnp.int32).astype(jnp.float32)
    sign = jnp.clip(level, -1.0, 1.0)
    return sign * jnp.exp2(jnp.abs(level) * (1.0 / CODE_STEPS) - CODE_LOW)


def fold(v):
    half = v.shape[1] // 2
    return jnp.concatenate([v[:, :half], v[:, half:]], axis=0)


def unfold(v):
    half = v.shape[0] // 2
    return jnp.concatenate([v[:half], v[half:]], axis=1)


def kernel(
    mate_bit,
    pair_slots,
    units,
    x_ref,
    g_ref,
    params_ref,
    moment_ref,
    new_params,
    new_moment,
    x_own,
    x_near,
    xt_own,
    xt_near,
    g_own,
    g_near,
    p_own,
    m_own,
    part,
    ring_out,
    ring_in,
    total,
    fin_out,
    fin_in,
    mate_out,
    mate_in,
    x_sem,
    g_sem,
    pm_sem,
    near_send,
    near_recv,
    ring_send,
    ring_recv,
    fin_send,
    fin_recv,
    mate_send,
    mate_recv,
):
    n_pair = len(pair_slots)
    n_flat = units - n_pair
    group = lax.axis_index("group")
    index = lax.axis_index("fsdp")
    z = index % NZ_RING
    side = index // NZ_RING
    near = (group, (1 - side) * NZ_RING + z)
    low = group // 2**mate_bit % 2
    mate = (group + (1 - 2 * low) * 2**mate_bit, index)

    def along(step):
        return (group, side * NZ_RING + (z + step + NZ_RING) % NZ_RING)

    def pair_number(u):
        return sum((u > t).astype(jnp.int32) for t in pair_slots)

    def is_pair(u):
        return sum((u == t).astype(jnp.int32) for t in pair_slots) == 1

    def flat_col(u):
        return pl.multiple_of((u - pair_number(u)) * C, C)

    def pair_col(which, j):
        return pl.multiple_of((n_flat + which * n_pair + j) * C, C)

    def load_g(u, col):
        return pltpu.make_async_copy(
            g_ref.at[:, pl.ds(col, C)], g_own.at[u], g_sem.at[u]
        )

    def own_col(u):
        pair = is_pair(u).astype(jnp.int32)
        j = pair_number(u)
        return pl.multiple_of(
            pair * (n_flat + side * n_pair + j) * C + (1 - pair) * (u - j) * C, C
        )

    load_x = pltpu.make_async_copy(x_ref, x_own, x_sem)
    load_x.start()

    @pl.loop(0, units)
    def _(u):
        load_g(u, own_col(u)).start()

    load_p = pltpu.make_async_copy(params_ref.at[0], p_own, pm_sem.at[0])
    load_m = pltpu.make_async_copy(moment_ref.at[0], m_own, pm_sem.at[1])
    load_p.start()
    load_m.start()

    barrier = pltpu.get_barrier_semaphore()
    for device in (along(1), along(-1), near, mate):
        pl.semaphore_signal(barrier, inc=1, device_id=device, device_id_type=MESH)
    pl.semaphore_wait(barrier, 4)

    send_x = pltpu.make_async_remote_copy(
        src_ref=x_ref,
        dst_ref=x_near,
        send_sem=near_send.at[n_pair],
        recv_sem=near_recv.at[n_pair],
        device_id=near,
        device_id_type=MESH,
    )
    send_x.start()

    def send_g(j):
        return pltpu.make_async_remote_copy(
            src_ref=g_ref.at[:, pl.ds(pair_col(1 - side, j), C)],
            dst_ref=g_near.at[j],
            send_sem=near_send.at[j],
            recv_sem=near_recv.at[j],
            device_id=near,
            device_id_type=MESH,
        )

    for j in range(AHEAD):
        send_g(j).start()

    load_x.wait()
    xt_own[...] = x_own[...].astype(jnp.float32).T.astype(jnp.bfloat16)

    def ring(u, k, step):
        return pltpu.make_async_remote_copy(
            src_ref=ring_out.at[u, k],
            dst_ref=ring_in.at[u, k],
            send_sem=ring_send.at[u, k],
            recv_sem=ring_recv.at[u, k],
            device_id=along(step),
            device_id_type=MESH,
        )

    def own_rows(u, where):
        first = pl.multiple_of(where * ROWS, 8)
        second = pl.multiple_of(NZ_RING * ROWS + where * ROWS, 8)
        return jnp.concatenate(
            [part[u, pl.ds(first, ROWS), :], part[u, pl.ds(second, ROWS), :]], axis=0
        )

    def turn(u):
        return 1 - 2 * (u % 2)

    def place(u, distance):
        return (z + turn(u) * distance + NZ_RING) % NZ_RING

    def start(u):
        pair = is_pair(u)
        j = pair_number(u)

        @pl.when(jnp.logical_not(pair))
        def _():
            load_g(u, own_col(u)).wait()
            part[u] = jnp.dot(
                xt_own[...], g_own[u], preferred_element_type=jnp.float32
            )

        @pl.when(pair)
        def _():
            load_g(u, own_col(u)).wait()

            @pl.when(j == 0)
            def _():
                send_x.wait_recv()
                xt_near[...] = x_near[...].astype(jnp.float32).T.astype(jnp.bfloat16)

            send_g(j).wait_recv()

            @pl.when(j + AHEAD < n_pair)
            def _():
                send_g(j + AHEAD).start()

            part[u] = jnp.dot(
                xt_own[...], g_own[u], preferred_element_type=jnp.float32
            ) + jnp.dot(xt_near[...], g_near[j], preferred_element_type=jnp.float32)

        ring_out[u, 0] = encode(own_rows(u, place(u, 4)))
        ring(u, 0, turn(u)).start()
        ring_out[u, 4] = encode(own_rows(u, place(u, -3)))
        ring(u, 4, -turn(u)).start()

    def hop(h, u):
        ring(u, h - 1, turn(u)).wait_recv()
        ring_out[u, h] = encode(decode(ring_in[u, h - 1]) + own_rows(u, place(u, 4 - h)))
        ring(u, h, turn(u)).start()
        if h < 3:
            ring(u, h + 3, -turn(u)).wait_recv()
            ring_out[u, h + 4] = encode(
                decode(ring_in[u, h + 3]) + own_rows(u, place(u, h - 3))
            )
            ring(u, h + 4, -turn(u)).start()

    def fin(u):
        return pltpu.make_async_remote_copy(
            src_ref=fin_out.at[u],
            dst_ref=fin_in.at[u],
            send_sem=fin_send.at[u],
            recv_sem=fin_recv.at[u],
            device_id=near,
            device_id_type=MESH,
        )

    def finish(u):
        ring(u, 6, -turn(u)).wait_recv()
        ring(u, 3, turn(u)).wait_recv()
        total[u] = decode(ring_in[u, 3]) + decode(ring_in[u, 6]) + own_rows(u, z)
        other = total[u, pl.ds(pl.multiple_of((1 - side) * ROWS, 8), ROWS), :]
        fin_out[u] = encode(fold(other))
        fin(u).start()

    def mate_flat(u):
        return pltpu.make_async_remote_copy(
            src_ref=mate_out.at[u, :, pl.ds(0, C // 2)],
            dst_ref=mate_in.at[u, :, pl.ds(0, C // 2)],
            send_sem=mate_send.at[u],
            recv_sem=mate_recv.at[u],
            device_id=mate,
            device_id_type=MESH,
        )

    def mate_pair(u):
        return pltpu.make_async_remote_copy(
            src_ref=mate_out.at[u],
            dst_ref=mate_in.at[u],
            send_sem=mate_send.at[u],
            recv_sem=mate_recv.at[u],
            device_id=mate,
            device_id_type=MESH,
        )

    def step(col, grad):
        columns = pl.ds(col, C)
        moved = MOMENTUM * m_own[:, columns] + grad
        half = p_own[:, columns] - RATE * (grad + MOMENTUM * moved)
        new_moment[0, :, columns] = moved
        new_params[0, :, columns] = half
        return half

    def update(u):
        @pl.when(u == 0)
        def _():
            load_p.wait()
            load_m.wait()

        fin(u).wait_recv()
        near_sum = unfold(decode(fin_in[u]))
        own_sum = total[u, pl.ds(pl.multiple_of(side * ROWS, 8), ROWS), :]
        pair = is_pair(u)
        j = pair_number(u)

        @pl.when(jnp.logical_not(pair))
        def _():
            half = step(flat_col(u), own_sum + near_sum)
            mate_out[u, :, : C // 2] = encode(fold(half))
            mate_flat(u).start()

        @pl.when(pair)
        def _():
            own_half = step(pair_col(side, j), own_sum)
            near_half = step(pair_col(1 - side, j), near_sum)
            mate_out[u] = encode(jnp.concatenate([own_half, near_half], axis=0))
            mate_pair(u).start()

    def average(u):
        pair = is_pair(u)
        j = pair_number(u)

        @pl.when(jnp.logical_not(pair))
        def _():
            mate_flat(u).wait_recv()
            columns = pl.ds(flat_col(u), C)
            got = unfold(decode(mate_in[u, :, : C // 2]))
            new_params[0, :, columns] = 0.5 * (new_params[0, :, columns] + got)

        @pl.when(pair)
        def _():
            mate_pair(u).wait_recv()
            got = decode(mate_in[u])
            columns = pl.ds(pair_col(side, j), C)
            new_params[0, :, columns] = 0.5 * (new_params[0, :, columns] + got[:ROWS])
            columns = pl.ds(pair_col(1 - side, j), C)
            new_params[0, :, columns] = 0.5 * (new_params[0, :, columns] + got[ROWS:])

    stages = [(HOP_LAG * h, partial(hop, h)) for h in (3, 2, 1)]
    stages += [(0, start), (4 * HOP_LAG, finish)]
    stages += [(4 * HOP_LAG + FIN_LAG, update)]
    last = 4 * HOP_LAG + FIN_LAG + MATE_LAG
    stages += [(last, average)]

    @pl.loop(0, units + last)
    def _(s):
        for lag, stage in stages:
            u = s - lag

            @pl.when(jnp.logical_and(u >= 0, u < units))
            def _():
                stage(u)

    send_x.wait_send()

    @pl.loop(0, n_pair)
    def _(j):
        send_g(j).wait_send()

    @pl.loop(0, units)
    def _(u):
        for k in range(4):
            ring(u, k, 1).wait_send()
        for k in range(4, 7):
            ring(u, k, -1).wait_send()
        fin(u).wait_send()

        @pl.when(is_pair(u))
        def _():
            mate_pair(u).wait_send()

        @pl.when(jnp.logical_not(is_pair(u)))
        def _():
            mate_flat(u).wait_send()


def run(mate_bit, pair_slots, units, activations, cotangent, params, moment):
    n_pair = len(pair_slots)
    any_ref = pl.BlockSpec(memory_space=pl.ANY)
    vmem_ref = pl.BlockSpec(memory_space=pltpu.VMEM)
    dma = pltpu.SemaphoreType.DMA
    bf16, f32, i16 = jnp.bfloat16, jnp.float32, jnp.int16
    out = jax.ShapeDtypeStruct((1, ROWS, HID), f32)
    return pl.pallas_call(
        partial(kernel, mate_bit, pair_slots, units),
        out_shape=(out, out),
        in_specs=[any_ref] * 4,
        out_specs=(vmem_ref, vmem_ref),
        scratch_shapes=[
            pltpu.VMEM((TOK, WROWS), bf16),
            pltpu.VMEM((TOK, WROWS), bf16),
            pltpu.VMEM((WROWS, TOK), bf16),
            pltpu.VMEM((WROWS, TOK), bf16),
            pltpu.VMEM((units, TOK, C), bf16),
            pltpu.VMEM((n_pair, TOK, C), bf16),
            pltpu.VMEM((ROWS, HID), f32),
            pltpu.VMEM((ROWS, HID), f32),
            pltpu.VMEM((units, WROWS, C), f32),
            pltpu.VMEM((units, 7, 2 * ROWS, C), i16),
            pltpu.VMEM((units, 7, 2 * ROWS, C), i16),
            pltpu.VMEM((units, 2 * ROWS, C), f32),
            pltpu.VMEM((units, 2 * ROWS, C // 2), i16),
            pltpu.VMEM((units, 2 * ROWS, C // 2), i16),
            pltpu.VMEM((units, 2 * ROWS, C), i16),
            pltpu.VMEM((units, 2 * ROWS, C), i16),
            dma,
            dma((units,)),
            dma((2,)),
            dma((n_pair + 1,)),
            dma((n_pair + 1,)),
            dma((units, 7)),
            dma((units, 7)),
            dma((units,)),
            dma((units,)),
            dma((units,)),
            dma((units,)),
        ],
        compiler_params=pltpu.CompilerParams(
            collective_id=mate_bit, has_side_effects=True, vmem_limit_bytes=60 << 20
        ),
        cost_estimate=pl.CostEstimate(
            flops=2 * TOK * WROWS * HID, bytes_accessed=13 << 20, transcendentals=0
        ),
    )(activations, cotangent, params, moment)


def on_device(activations, cotangent, params, moment, step_index):
    bits = lax.axis_size("group").bit_length() - 1
    branches = [partial(run, bit, PAIR_SLOTS, UNITS) for bit in range(bits)]
    return lax.switch(
        step_index % bits, branches, activations, cotangent, params, moment
    )


def solution(mesh):
    in_specs = (
        P(("group", "fsdp"), None),
        P(("group", "fsdp"), None),
        P("group", "fsdp", None),
        P("group", "fsdp", None),
        P(),
    )
    out_specs = (P("group", "fsdp", None), P("group", "fsdp", None))
    return jax.shard_map(
        on_device, mesh=mesh, in_specs=in_specs, out_specs=out_specs, check_vma=False
    )
```

```python
from functools import partial

import jax
import jax.numpy as jnp
from jax import lax
from jax.experimental import pallas as pl
from jax.experimental.pallas import tpu as pltpu
from jax.sharding import PartitionSpec as P

RATE = 0.1
MOMENTUM = 0.9

HID = 14336
TOK = 256
WROWS = 384
ROWS = 24
NZ_RING = 8
C = 512

CODE_LOW = 30.0
CODE_HIGH = 11.2
CODE_STEPS = 32766.0 / (CODE_LOW + CODE_HIGH)
CODE_TINY = 2.0**-30

MESH = pl.DeviceIdType.MESH
PAIR_SLOTS = (6, 7, 9, 10, 12, 13, 15, 17, 18)
UNITS = 28 - len(PAIR_SLOTS)
LAGS = (2, 4, 7, 11, 14, 18)
ORDER = (3, 1, 2, 0, 4, 5, 6)
DRAIN_LAG = 1
AHEAD = 2
EARLY = 3


def encode(v):
    size = jnp.maximum(jnp.abs(v), CODE_TINY)
    level = jnp.log2(size) * CODE_STEPS + (CODE_LOW * CODE_STEPS + 0.5)
    return jnp.where(v < 0.0, -level, level).astype(jnp.int32).astype(jnp.int16)


def decode(q):
    level = q.astype(jnp.int32).astype(jnp.float32)
    sign = jnp.clip(level, -1.0, 1.0)
    return sign * jnp.exp2(jnp.abs(level) * (1.0 / CODE_STEPS) - CODE_LOW)


def fold(v):
    half = v.shape[1] // 2
    return jnp.concatenate([v[:, :half], v[:, half:]], axis=0)


def unfold(v):
    half = v.shape[0] // 2
    return jnp.concatenate([v[:half], v[half:]], axis=1)


def kernel(
    mate_bit,
    pair_slots,
    units,
    x_ref,
    g_ref,
    params_ref,
    moment_ref,
    new_params_ref,
    new_moment_ref,
    new_params,
    new_moment,
    x_own,
    x_near,
    xt_own,
    xt_near,
    g_own,
    g_near,
    p_own,
    m_own,
    part,
    ring_out,
    ring_in,
    total,
    fin_out,
    fin_in,
    mate_out,
    mate_in,
    x_sem,
    g_sem,
    pm_sem,
    near_send,
    near_recv,
    ring_send,
    ring_recv,
    fin_send,
    fin_recv,
    mate_send,
    mate_recv,
    out_sem,
):
    n_pair = len(pair_slots)
    n_flat = units - n_pair
    group = lax.axis_index("group")
    index = lax.axis_index("fsdp")
    z = index % NZ_RING
    side = index // NZ_RING
    near = (group, (1 - side) * NZ_RING + z)
    low = group // 2**mate_bit % 2
    mate = (group + (1 - 2 * low) * 2**mate_bit, index)

    def along(step):
        return (group, side * NZ_RING + (z + step + NZ_RING) % NZ_RING)

    def pair_number(u):
        return sum((u > t).astype(jnp.int32) for t in pair_slots)

    def is_pair(u):
        return sum((u == t).astype(jnp.int32) for t in pair_slots) == 1

    def flat_col(u):
        return pl.multiple_of((u - pair_number(u)) * C, C)

    def pair_col(which, j):
        return pl.multiple_of((n_flat + which * n_pair + j) * C, C)

    def load_g(u, col):
        return pltpu.make_async_copy(
            g_ref.at[:, pl.ds(col, C)], g_own.at[u], g_sem.at[u]
        )

    def own_col(u):
        pair = is_pair(u).astype(jnp.int32)
        j = pair_number(u)
        return pl.multiple_of(
            pair * (n_flat + side * n_pair + j) * C + (1 - pair) * (u - j) * C, C
        )

    barrier = pltpu.get_barrier_semaphore()
    for device in (along(1), along(-1), near, mate):
        pl.semaphore_signal(barrier, inc=1, device_id=device, device_id_type=MESH)

    load_x = pltpu.make_async_copy(x_ref, x_own, x_sem)
    load_x.start()

    @pl.loop(0, units)
    def _(u):
        load_g(u, own_col(u)).start()

    load_p = pltpu.make_async_copy(params_ref.at[0], p_own, pm_sem.at[0])
    load_m = pltpu.make_async_copy(moment_ref.at[0], m_own, pm_sem.at[1])
    load_p.start()
    load_m.start()

    send_x = pltpu.make_async_remote_copy(
        src_ref=x_ref,
        dst_ref=x_near,
        send_sem=near_send.at[n_pair],
        recv_sem=near_recv.at[n_pair],
        device_id=near,
        device_id_type=MESH,
    )

    def send_g(j):
        return pltpu.make_async_remote_copy(
            src_ref=g_ref.at[:, pl.ds(pair_col(1 - side, j), C)],
            dst_ref=g_near.at[j],
            send_sem=near_send.at[j],
            recv_sem=near_recv.at[j],
            device_id=near,
            device_id_type=MESH,
        )

    def ring(u, k, step):
        return pltpu.make_async_remote_copy(
            src_ref=ring_out.at[u, k],
            dst_ref=ring_in.at[u, k],
            send_sem=ring_send.at[u, k],
            recv_sem=ring_recv.at[u, k],
            device_id=along(step),
            device_id_type=MESH,
        )

    def own_rows(u, where):
        first = pl.multiple_of(where * ROWS, 8)
        second = pl.multiple_of(NZ_RING * ROWS + where * ROWS, 8)
        return jnp.concatenate(
            [part[u, pl.ds(first, ROWS), :], part[u, pl.ds(second, ROWS), :]], axis=0
        )

    def turn(u):
        return 1 - 2 * (u % 2)

    def place(u, distance):
        return (z + turn(u) * distance + NZ_RING) % NZ_RING

    def form_flat(u):
        load_g(u, own_col(u)).wait()
        part[u] = jnp.dot(xt_own[...], g_own[u], preferred_element_type=jnp.float32)

    def form_pair(u):
        j = pair_number(u)
        load_g(u, own_col(u)).wait()

        @pl.when(j == 0)
        def _():
            send_x.wait_recv()
            xt_near[...] = x_near[...].astype(jnp.float32).T.astype(jnp.bfloat16)

        send_g(j).wait_recv()

        @pl.when(j + AHEAD < n_pair)
        def _():
            send_g(j + AHEAD).start()

        part[u] = jnp.dot(
            xt_own[...], g_own[u], preferred_element_type=jnp.float32
        ) + jnp.dot(xt_near[...], g_near[j], preferred_element_type=jnp.float32)

    def first_codes(u):
        ring_out[u, 0] = encode(own_rows(u, place(u, 4)))
        ring_out[u, 4] = encode(own_rows(u, place(u, -3)))

    def launch(u):
        ring(u, 0, turn(u)).start()
        ring(u, 4, -turn(u)).start()

    def start(u):
        @pl.when(u >= EARLY)
        def _():
            pair = is_pair(u)
            pl.when(jnp.logical_not(pair))(lambda: form_flat(u))
            pl.when(pair)(lambda: form_pair(u))
            first_codes(u)
            launch(u)

    def hop(h, u):
        ring(u, h - 1, turn(u)).wait_recv()
        ring_out[u, h] = encode(decode(ring_in[u, h - 1]) + own_rows(u, place(u, 4 - h)))
        ring(u, h, turn(u)).start()
        if h < 3:
            ring(u, h + 3, -turn(u)).wait_recv()
            ring_out[u, h + 4] = encode(
                decode(ring_in[u, h + 3]) + own_rows(u, place(u, h - 3))
            )
            ring(u, h + 4, -turn(u)).start()

    def fin(u):
        return pltpu.make_async_remote_copy(
            src_ref=fin_out.at[u],
            dst_ref=fin_in.at[u],
            send_sem=fin_send.at[u],
            recv_sem=fin_recv.at[u],
            device_id=near,
            device_id_type=MESH,
        )

    def finish(u):
        ring(u, 6, -turn(u)).wait_recv()
        ring(u, 3, turn(u)).wait_recv()
        total[u] = decode(ring_in[u, 3]) + decode(ring_in[u, 6]) + own_rows(u, z)
        other = total[u, pl.ds(pl.multiple_of((1 - side) * ROWS, 8), ROWS), :]
        fin_out[u] = encode(fold(other))
        fin(u).start()

    def mate_flat(u):
        return pltpu.make_async_remote_copy(
            src_ref=mate_out.at[u, :, pl.ds(0, C // 2)],
            dst_ref=mate_in.at[u, :, pl.ds(0, C // 2)],
            send_sem=mate_send.at[u],
            recv_sem=mate_recv.at[u],
            device_id=mate,
            device_id_type=MESH,
        )

    def mate_pair(u):
        return pltpu.make_async_remote_copy(
            src_ref=mate_out.at[u],
            dst_ref=mate_in.at[u],
            send_sem=mate_send.at[u],
            recv_sem=mate_recv.at[u],
            device_id=mate,
            device_id_type=MESH,
        )

    def out_moment(u, which, col):
        columns = pl.ds(col, C)
        return pltpu.make_async_copy(
            new_moment.at[:, columns],
            new_moment_ref.at[0, :, columns],
            out_sem.at[u, which],
        )

    def out_params(u, which, col):
        columns = pl.ds(col, C)
        return pltpu.make_async_copy(
            new_params.at[:, columns],
            new_params_ref.at[0, :, columns],
            out_sem.at[u, 2 + which],
        )

    def step(u, which, col, grad):
        columns = pl.ds(col, C)
        moved = MOMENTUM * m_own[:, columns] + grad
        half = p_own[:, columns] - RATE * (grad + MOMENTUM * moved)
        new_moment[:, columns] = moved
        new_params[:, columns] = half
        out_moment(u, which, col).start()
        return half

    def mix(u, which, col, got):
        columns = pl.ds(col, C)
        new_params[:, columns] = 0.5 * (new_params[:, columns] + got)
        out_params(u, which, col).start()

    def update(u):
        @pl.when(u == 0)
        def _():
            load_p.wait()
            load_m.wait()

        fin(u).wait_recv()
        near_sum = unfold(decode(fin_in[u]))
        own_sum = total[u, pl.ds(pl.multiple_of(side * ROWS, 8), ROWS), :]
        pair = is_pair(u)
        j = pair_number(u)

        @pl.when(jnp.logical_not(pair))
        def _():
            half = step(u, 0, flat_col(u), own_sum + near_sum)
            mate_out[u, :, : C // 2] = encode(fold(half))
            mate_flat(u).start()

        @pl.when(pair)
        def _():
            own_half = step(u, 0, pair_col(side, j), own_sum)
            near_half = step(u, 1, pair_col(1 - side, j), near_sum)
            mate_out[u] = encode(jnp.concatenate([own_half, near_half], axis=0))
            mate_pair(u).start()

    def average(u):
        pair = is_pair(u)
        j = pair_number(u)

        @pl.when(jnp.logical_not(pair))
        def _():
            mate_flat(u).wait_recv()
            mix(u, 0, flat_col(u), unfold(decode(mate_in[u, :, : C // 2])))

        @pl.when(pair)
        def _():
            mate_pair(u).wait_recv()
            got = decode(mate_in[u])
            mix(u, 0, pair_col(side, j), got[:ROWS])
            mix(u, 1, pair_col(1 - side, j), got[ROWS:])

    def drain(u):
        for k in range(4):
            ring(u, k, 1).wait_send()
        for k in range(4, 7):
            ring(u, k, -1).wait_send()
        fin(u).wait_send()
        pair = is_pair(u)
        j = pair_number(u)

        @pl.when(pair)
        def _():
            send_g(j).wait_send()
            mate_pair(u).wait_send()
            for which, col in ((0, pair_col(side, j)), (1, pair_col(1 - side, j))):
                out_moment(u, which, col).wait()
                out_params(u, which, col).wait()

        @pl.when(jnp.logical_not(pair))
        def _():
            mate_flat(u).wait_send()
            out_moment(u, 0, flat_col(u)).wait()
            out_params(u, 0, flat_col(u)).wait()

    load_x.wait()
    xt_own[...] = x_own[...].astype(jnp.float32).T.astype(jnp.bfloat16)

    @pl.loop(0, EARLY)
    def _(u):
        form_flat(u)
        first_codes(u)

    pl.semaphore_wait(barrier, 4)
    send_x.start()

    @pl.loop(0, EARLY)
    def _(u):
        launch(u)

    for j in range(AHEAD):
        send_g(j).start()

    actions = (start, partial(hop, 1), partial(hop, 2), partial(hop, 3))
    actions += (finish, update, average)
    lags = (0, *LAGS)
    last = lags[-1]
    stages = [(lags[k], actions[k]) for k in ORDER] + [(last + DRAIN_LAG, drain)]

    @pl.loop(0, units + last + DRAIN_LAG)
    def _(s):
        for lag, stage in stages:
            u = s - lag

            @pl.when(jnp.logical_and(u >= 0, u < units))
            def _():
                stage(u)

    send_x.wait_send()


def run(mate_bit, pair_slots, units, activations, cotangent, params, moment):
    n_pair = len(pair_slots)
    any_ref = pl.BlockSpec(memory_space=pl.ANY)
    dma = pltpu.SemaphoreType.DMA
    bf16, f32, i16 = jnp.bfloat16, jnp.float32, jnp.int16
    out = jax.ShapeDtypeStruct((1, ROWS, HID), f32)
    return pl.pallas_call(
        partial(kernel, mate_bit, pair_slots, units),
        out_shape=(out, out),
        in_specs=[any_ref] * 4,
        out_specs=(any_ref, any_ref),
        scratch_shapes=[
            pltpu.VMEM((ROWS, HID), f32),
            pltpu.VMEM((ROWS, HID), f32),
            pltpu.VMEM((TOK, WROWS), bf16),
            pltpu.VMEM((TOK, WROWS), bf16),
            pltpu.VMEM((WROWS, TOK), bf16),
            pltpu.VMEM((WROWS, TOK), bf16),
            pltpu.VMEM((units, TOK, C), bf16),
            pltpu.VMEM((n_pair, TOK, C), bf16),
            pltpu.VMEM((ROWS, HID), f32),
            pltpu.VMEM((ROWS, HID), f32),
            pltpu.VMEM((units, WROWS, C), f32),
            pltpu.VMEM((units, 7, 2 * ROWS, C), i16),
            pltpu.VMEM((units, 7, 2 * ROWS, C), i16),
            pltpu.VMEM((units, 2 * ROWS, C), f32),
            pltpu.VMEM((units, 2 * ROWS, C // 2), i16),
            pltpu.VMEM((units, 2 * ROWS, C // 2), i16),
            pltpu.VMEM((units, 2 * ROWS, C), i16),
            pltpu.VMEM((units, 2 * ROWS, C), i16),
            dma,
            dma((units,)),
            dma((2,)),
            dma((n_pair + 1,)),
            dma((n_pair + 1,)),
            dma((units, 7)),
            dma((units, 7)),
            dma((units,)),
            dma((units,)),
            dma((units,)),
            dma((units,)),
            dma((units, 4)),
        ],
        compiler_params=pltpu.CompilerParams(
            collective_id=mate_bit, has_side_effects=True, vmem_limit_bytes=60 << 20
        ),
        cost_estimate=pl.CostEstimate(
            flops=2 * TOK * WROWS * HID, bytes_accessed=13 << 20, transcendentals=0
        ),
    )(activations, cotangent, params, moment)


def on_device(activations, cotangent, params, moment, step_index):
    bits = lax.axis_size("group").bit_length() - 1
    branches = [partial(run, bit, PAIR_SLOTS, UNITS) for bit in range(bits)]
    return lax.switch(
        step_index % bits, branches, activations, cotangent, params, moment
    )


def solution(mesh):
    in_specs = (
        P(("group", "fsdp"), None),
        P(("group", "fsdp"), None),
        P("group", "fsdp", None),
        P("group", "fsdp", None),
        P(),
    )
    out_specs = (P("group", "fsdp", None), P("group", "fsdp", None))
    return jax.shard_map(
        on_device, mesh=mesh, in_specs=in_specs, out_specs=out_specs, check_vma=False
    )
```

```python
from functools import partial

import jax
import jax.numpy as jnp
from jax import lax
from jax.experimental import pallas as pl
from jax.experimental.pallas import tpu as pltpu
from jax.sharding import PartitionSpec as P

RATE = 0.1
MOMENTUM = 0.9

HID = 14336
TOK = 256
WROWS = 384
ROWS = 24
NZ_RING = 8
C = 512

CODE_LOW = 30.0
CODE_HIGH = 11.2
CODE_STEPS = 32766.0 / (CODE_LOW + CODE_HIGH)
CODE_TINY = 2.0**-30

MESH = pl.DeviceIdType.MESH
PAIR_SLOTS = (6, 7, 9, 10, 12, 13, 15, 17, 18)
UNITS = 28 - len(PAIR_SLOTS)
LAGS = (2, 4, 7, 10, 13, 17)
ORDER = (3, 1, 2, 0, 4, 5, 6)
DRAIN_LAG = 1
FIN_FROM = 0
UPDATE_FROM = 0
LATE = 1
AHEAD = 2
EARLY = 3


def encode(v):
    size = jnp.maximum(jnp.abs(v), CODE_TINY)
    level = jnp.log2(size) * CODE_STEPS + (CODE_LOW * CODE_STEPS + 0.5)
    return jnp.where(v < 0.0, -level, level).astype(jnp.int32).astype(jnp.int16)


def decode(q):
    level = q.astype(jnp.int32).astype(jnp.float32)
    sign = jnp.clip(level, -1.0, 1.0)
    return sign * jnp.exp2(jnp.abs(level) * (1.0 / CODE_STEPS) - CODE_LOW)


def fold(v):
    half = v.shape[1] // 2
    return jnp.concatenate([v[:, :half], v[:, half:]], axis=0)


def unfold(v):
    half = v.shape[0] // 2
    return jnp.concatenate([v[:half], v[half:]], axis=1)


def kernel(
    mate_bit,
    pair_slots,
    units,
    x_ref,
    g_ref,
    params_ref,
    moment_ref,
    new_params_ref,
    new_moment_ref,
    new_params,
    new_moment,
    x_own,
    x_near,
    xt_own,
    xt_near,
    g_own,
    g_near,
    p_own,
    m_own,
    part,
    ring_out,
    ring_in,
    total,
    fin_out,
    fin_in,
    cross_in,
    mate_out,
    mate_in,
    x_sem,
    g_sem,
    pm_sem,
    near_send,
    near_recv,
    ring_send,
    ring_recv,
    fin_send,
    fin_recv,
    cross_send,
    cross_recv,
    mate_send,
    mate_recv,
    out_sem,
):
    n_pair = len(pair_slots)
    n_flat = units - n_pair
    group = lax.axis_index("group")
    index = lax.axis_index("fsdp")
    z = index % NZ_RING
    side = index // NZ_RING
    near = (group, (1 - side) * NZ_RING + z)
    low = group // 2**mate_bit % 2
    mate = (group + (1 - 2 * low) * 2**mate_bit, index)
    cross = (mate[0], near[1])

    def along(step):
        return (group, side * NZ_RING + (z + step + NZ_RING) % NZ_RING)

    def pair_number(u):
        return sum((u > t).astype(jnp.int32) for t in pair_slots)

    def is_pair(u):
        return sum((u == t).astype(jnp.int32) for t in pair_slots) == 1

    def flat_col(u):
        return pl.multiple_of((u - pair_number(u)) * C, C)

    def pair_col(which, j):
        return pl.multiple_of((n_flat + which * n_pair + j) * C, C)

    def load_g(u, col):
        return pltpu.make_async_copy(
            g_ref.at[:, pl.ds(col, C)], g_own.at[u], g_sem.at[u]
        )

    def own_col(u):
        pair = is_pair(u).astype(jnp.int32)
        j = pair_number(u)
        return pl.multiple_of(
            pair * (n_flat + side * n_pair + j) * C + (1 - pair) * (u - j) * C, C
        )

    barrier = pltpu.get_barrier_semaphore()
    for device in (along(1), along(-1), near, mate, cross):
        pl.semaphore_signal(barrier, inc=1, device_id=device, device_id_type=MESH)

    load_x = pltpu.make_async_copy(x_ref, x_own, x_sem)
    load_x.start()

    @pl.loop(0, units)
    def _(u):
        load_g(u, own_col(u)).start()

    load_p = pltpu.make_async_copy(params_ref.at[0], p_own, pm_sem.at[0])
    load_m = pltpu.make_async_copy(moment_ref.at[0], m_own, pm_sem.at[1])
    load_p.start()
    load_m.start()

    send_x = pltpu.make_async_remote_copy(
        src_ref=x_ref,
        dst_ref=x_near,
        send_sem=near_send.at[n_pair],
        recv_sem=near_recv.at[n_pair],
        device_id=near,
        device_id_type=MESH,
    )

    def send_g(j):
        return pltpu.make_async_remote_copy(
            src_ref=g_ref.at[:, pl.ds(pair_col(1 - side, j), C)],
            dst_ref=g_near.at[j],
            send_sem=near_send.at[j],
            recv_sem=near_recv.at[j],
            device_id=near,
            device_id_type=MESH,
        )

    def ring(u, k, step):
        return pltpu.make_async_remote_copy(
            src_ref=ring_out.at[u, k],
            dst_ref=ring_in.at[u, k],
            send_sem=ring_send.at[u, k],
            recv_sem=ring_recv.at[u, k],
            device_id=along(step),
            device_id_type=MESH,
        )

    def own_rows(u, where):
        first = pl.multiple_of(where * ROWS, 8)
        second = pl.multiple_of(NZ_RING * ROWS + where * ROWS, 8)
        return jnp.concatenate(
            [part[u, pl.ds(first, ROWS), :], part[u, pl.ds(second, ROWS), :]], axis=0
        )

    def turn(u):
        return 1 - 2 * (u % 2)

    def place(u, distance):
        return (z + turn(u) * distance + NZ_RING) % NZ_RING

    def form_flat(u):
        load_g(u, own_col(u)).wait()
        part[u] = jnp.dot(xt_own[...], g_own[u], preferred_element_type=jnp.float32)

    def form_pair(u):
        j = pair_number(u)
        load_g(u, own_col(u)).wait()

        @pl.when(j == 0)
        def _():
            send_x.wait_recv()
            xt_near[...] = x_near[...].astype(jnp.float32).T.astype(jnp.bfloat16)

        send_g(j).wait_recv()

        @pl.when(j + AHEAD < n_pair)
        def _():
            send_g(j + AHEAD).start()

        part[u] = jnp.dot(
            xt_own[...], g_own[u], preferred_element_type=jnp.float32
        ) + jnp.dot(xt_near[...], g_near[j], preferred_element_type=jnp.float32)

    def first_codes(u):
        ring_out[u, 0] = encode(own_rows(u, place(u, 4)))
        ring_out[u, 4] = encode(own_rows(u, place(u, -3)))

    def launch(u):
        ring(u, 0, turn(u)).start()
        ring(u, 4, -turn(u)).start()

    def start(u):
        @pl.when(u >= EARLY)
        def _():
            pair = is_pair(u)
            pl.when(jnp.logical_not(pair))(lambda: form_flat(u))
            pl.when(pair)(lambda: form_pair(u))
            first_codes(u)
            launch(u)

    def hop(h, u):
        ring(u, h - 1, turn(u)).wait_recv()
        ring_out[u, h] = encode(decode(ring_in[u, h - 1]) + own_rows(u, place(u, 4 - h)))
        ring(u, h, turn(u)).start()
        if h < 3:
            ring(u, h + 3, -turn(u)).wait_recv()
            ring_out[u, h + 4] = encode(
                decode(ring_in[u, h + 3]) + own_rows(u, place(u, h - 3))
            )
            ring(u, h + 4, -turn(u)).start()

    def fin(u):
        return pltpu.make_async_remote_copy(
            src_ref=fin_out.at[u],
            dst_ref=fin_in.at[u],
            send_sem=fin_send.at[u],
            recv_sem=fin_recv.at[u],
            device_id=near,
            device_id_type=MESH,
        )

    def finish(u):
        ring(u, 6, -turn(u)).wait_recv()
        ring(u, 3, turn(u)).wait_recv()
        total[u] = decode(ring_in[u, 3]) + decode(ring_in[u, 6]) + own_rows(u, z)
        other = total[u, pl.ds(pl.multiple_of((1 - side) * ROWS, 8), ROWS), :]
        fin_out[u] = encode(fold(other))

        @pl.when(u >= units - LATE)
        def _():
            crossing(u).start()
            pair = is_pair(u)
            j = pair_number(u)
            own_sum = total[u, pl.ds(pl.multiple_of(side * ROWS, 8), ROWS), :]

            @pl.when(jnp.logical_not(pair))
            def _():
                half = half_of(flat_col(u), own_sum)
                mate_out[u, :, : C // 2] = encode(fold(half))
                mate_flat(u).start()

            @pl.when(pair)
            def _():
                own_half = half_of(pair_col(side, j), own_sum)
                near_half = half_of(pair_col(1 - side, j), jnp.zeros_like(own_sum))
                mate_out[u] = encode(jnp.concatenate([own_half, near_half], axis=0))
                mate_pair(u).start()

    def send_fin(u):
        fin(u).start()

    def crossing(u):
        return pltpu.make_async_remote_copy(
            src_ref=fin_out.at[u],
            dst_ref=cross_in.at[u - (units - LATE)],
            send_sem=cross_send.at[u - (units - LATE)],
            recv_sem=cross_recv.at[u - (units - LATE)],
            device_id=cross,
            device_id_type=MESH,
        )

    def mate_flat(u):
        return pltpu.make_async_remote_copy(
            src_ref=mate_out.at[u, :, pl.ds(0, C // 2)],
            dst_ref=mate_in.at[u, :, pl.ds(0, C // 2)],
            send_sem=mate_send.at[u],
            recv_sem=mate_recv.at[u],
            device_id=mate,
            device_id_type=MESH,
        )

    def mate_pair(u):
        return pltpu.make_async_remote_copy(
            src_ref=mate_out.at[u],
            dst_ref=mate_in.at[u],
            send_sem=mate_send.at[u],
            recv_sem=mate_recv.at[u],
            device_id=mate,
            device_id_type=MESH,
        )

    def out_moment(u, which, col):
        columns = pl.ds(col, C)
        return pltpu.make_async_copy(
            new_moment.at[:, columns],
            new_moment_ref.at[0, :, columns],
            out_sem.at[u, which],
        )

    def out_params(u, which, col):
        columns = pl.ds(col, C)
        return pltpu.make_async_copy(
            new_params.at[:, columns],
            new_params_ref.at[0, :, columns],
            out_sem.at[u, 2 + which],
        )

    def half_of(col, grad):
        columns = pl.ds(col, C)
        moved = MOMENTUM * m_own[:, columns] + grad
        return p_own[:, columns] - RATE * (grad + MOMENTUM * moved)

    def step(u, which, col, grad):
        columns = pl.ds(col, C)
        moved = MOMENTUM * m_own[:, columns] + grad
        half = p_own[:, columns] - RATE * (grad + MOMENTUM * moved)
        new_moment[:, columns] = moved
        new_params[:, columns] = half
        out_moment(u, which, col).start()
        return half

    def mix(u, which, col, got):
        columns = pl.ds(col, C)
        new_params[:, columns] = 0.5 * (new_params[:, columns] + got)
        out_params(u, which, col).start()

    def update(u):
        @pl.when(u == 0)
        def _():
            load_p.wait()
            load_m.wait()

        fin(u).wait_recv()
        near_sum = unfold(decode(fin_in[u]))
        own_sum = total[u, pl.ds(pl.multiple_of(side * ROWS, 8), ROWS), :]
        pair = is_pair(u)
        j = pair_number(u)
        late = u >= units - LATE
        soon = jnp.logical_not(late)

        @pl.when(late)
        def _():
            crossing(u).wait_recv()
            far = (RATE * (1.0 + MOMENTUM)) * unfold(
                decode(cross_in[u - (units - LATE)])
            )

            @pl.when(jnp.logical_not(pair))
            def _():
                col = flat_col(u)
                step(u, 0, col, own_sum + near_sum)
                mate_flat(u).wait_recv()
                mix(u, 0, col, unfold(decode(mate_in[u, :, : C // 2])) - far)

            @pl.when(pair)
            def _():
                step(u, 0, pair_col(side, j), own_sum)
                step(u, 1, pair_col(1 - side, j), near_sum)
                mate_pair(u).wait_recv()
                got = decode(mate_in[u])
                mix(u, 0, pair_col(side, j), got[:ROWS])
                mix(u, 1, pair_col(1 - side, j), got[ROWS:] - far)

        @pl.when(jnp.logical_and(soon, jnp.logical_not(pair)))
        def _():
            half = step(u, 0, flat_col(u), own_sum + near_sum)
            mate_out[u, :, : C // 2] = encode(fold(half))
            mate_flat(u).start()

        @pl.when(jnp.logical_and(soon, pair))
        def _():
            own_half = step(u, 0, pair_col(side, j), own_sum)
            near_half = step(u, 1, pair_col(1 - side, j), near_sum)
            mate_out[u] = encode(jnp.concatenate([own_half, near_half], axis=0))
            mate_pair(u).start()

    def average(u):
        pair = is_pair(u)
        j = pair_number(u)

        soon = u < units - LATE

        @pl.when(jnp.logical_and(soon, jnp.logical_not(pair)))
        def _():
            mate_flat(u).wait_recv()
            mix(u, 0, flat_col(u), unfold(decode(mate_in[u, :, : C // 2])))

        @pl.when(jnp.logical_and(soon, pair))
        def _():
            mate_pair(u).wait_recv()
            got = decode(mate_in[u])
            mix(u, 0, pair_col(side, j), got[:ROWS])
            mix(u, 1, pair_col(1 - side, j), got[ROWS:])

    def drain(u):
        for k in range(4):
            ring(u, k, 1).wait_send()
        for k in range(4, 7):
            ring(u, k, -1).wait_send()
        fin(u).wait_send()

        @pl.when(u >= units - LATE)
        def _():
            crossing(u).wait_send()

        pair = is_pair(u)
        j = pair_number(u)

        @pl.when(pair)
        def _():
            send_g(j).wait_send()
            mate_pair(u).wait_send()
            for which, col in ((0, pair_col(side, j)), (1, pair_col(1 - side, j))):
                out_moment(u, which, col).wait()
                out_params(u, which, col).wait()

        @pl.when(jnp.logical_not(pair))
        def _():
            mate_flat(u).wait_send()
            out_moment(u, 0, flat_col(u)).wait()
            out_params(u, 0, flat_col(u)).wait()

    load_x.wait()
    xt_own[...] = x_own[...].astype(jnp.float32).T.astype(jnp.bfloat16)

    @pl.loop(0, EARLY)
    def _(u):
        form_flat(u)
        first_codes(u)

    pl.semaphore_wait(barrier, 5)
    send_x.start()

    @pl.loop(0, EARLY)
    def _(u):
        launch(u)

    for j in range(AHEAD):
        send_g(j).start()

    actions = (start, partial(hop, 1), partial(hop, 2), partial(hop, 3))
    actions += (finish, update, average)
    lags = (0, *LAGS)
    last = lags[-1]

    def done(k, s):
        count = s + 1 - lags[k]
        if k == 5:
            count = jnp.minimum(count, 2 * (s + 1 - UPDATE_FROM))
        return jnp.clip(count, 0, units)

    def fins(s):
        return jnp.where(s < FIN_FROM, 0, jnp.clip(s + 1 - lags[4], 0, units))

    @pl.loop(0, units + last + DRAIN_LAG)
    def _(s):
        for k in ORDER:
            if k == 5:
                pl.loop(done(k, s - 1), done(k, s))(update)
                continue
            u = s - lags[k]
            pl.when(jnp.logical_and(u >= 0, u < units))(partial(actions[k], u))
            if k == 4:
                pl.loop(fins(s - 1), fins(s))(send_fin)
        u = s - last - DRAIN_LAG
        pl.when(u >= 0)(partial(drain, u))

    send_x.wait_send()


def run(mate_bit, pair_slots, units, activations, cotangent, params, moment):
    n_pair = len(pair_slots)
    any_ref = pl.BlockSpec(memory_space=pl.ANY)
    dma = pltpu.SemaphoreType.DMA
    bf16, f32, i16 = jnp.bfloat16, jnp.float32, jnp.int16
    out = jax.ShapeDtypeStruct((1, ROWS, HID), f32)
    return pl.pallas_call(
        partial(kernel, mate_bit, pair_slots, units),
        out_shape=(out, out),
        in_specs=[any_ref] * 4,
        out_specs=(any_ref, any_ref),
        scratch_shapes=[
            pltpu.VMEM((ROWS, HID), f32),
            pltpu.VMEM((ROWS, HID), f32),
            pltpu.VMEM((TOK, WROWS), bf16),
            pltpu.VMEM((TOK, WROWS), bf16),
            pltpu.VMEM((WROWS, TOK), bf16),
            pltpu.VMEM((WROWS, TOK), bf16),
            pltpu.VMEM((units, TOK, C), bf16),
            pltpu.VMEM((n_pair, TOK, C), bf16),
            pltpu.VMEM((ROWS, HID), f32),
            pltpu.VMEM((ROWS, HID), f32),
            pltpu.VMEM((units, WROWS, C), f32),
            pltpu.VMEM((units, 7, 2 * ROWS, C), i16),
            pltpu.VMEM((units, 7, 2 * ROWS, C), i16),
            pltpu.VMEM((units, 2 * ROWS, C), f32),
            pltpu.VMEM((units, 2 * ROWS, C // 2), i16),
            pltpu.VMEM((units, 2 * ROWS, C // 2), i16),
            pltpu.VMEM((LATE, 2 * ROWS, C // 2), i16),
            pltpu.VMEM((units, 2 * ROWS, C), i16),
            pltpu.VMEM((units, 2 * ROWS, C), i16),
            dma,
            dma((units,)),
            dma((2,)),
            dma((n_pair + 1,)),
            dma((n_pair + 1,)),
            dma((units, 7)),
            dma((units, 7)),
            dma((units,)),
            dma((units,)),
            dma((LATE,)),
            dma((LATE,)),
            dma((units,)),
            dma((units,)),
            dma((units, 4)),
        ],
        compiler_params=pltpu.CompilerParams(
            collective_id=mate_bit, has_side_effects=True, vmem_limit_bytes=50 << 20
        ),
        cost_estimate=pl.CostEstimate(
            flops=2 * TOK * WROWS * HID, bytes_accessed=13 << 20, transcendentals=0
        ),
    )(activations, cotangent, params, moment)


def on_device(activations, cotangent, params, moment, step_index):
    bits = lax.axis_size("group").bit_length() - 1
    branches = [partial(run, bit, PAIR_SLOTS, UNITS) for bit in range(bits)]
    return lax.switch(
        step_index % bits, branches, activations, cotangent, params, moment
    )


def solution(mesh):
    in_specs = (
        P(("group", "fsdp"), None),
        P(("group", "fsdp"), None),
        P("group", "fsdp", None),
        P("group", "fsdp", None),
        P(),
    )
    out_specs = (P("group", "fsdp", None), P("group", "fsdp", None))
    return jax.shard_map(
        on_device, mesh=mesh, in_specs=in_specs, out_specs=out_specs, check_vma=False
    )
```

```python
from functools import partial

import jax
import jax.numpy as jnp
from jax import lax
from jax.experimental import pallas as pl
from jax.experimental.pallas import tpu as pltpu
from jax.sharding import PartitionSpec as P

RATE = 0.1
MOMENTUM = 0.9

HID = 14336
TOK = 256
WROWS = 384
ROWS = 24
NZ_RING = 8
C = 512

CODE_LOW = 30.0
CODE_HIGH = 11.2
CODE_STEPS = 32766.0 / (CODE_LOW + CODE_HIGH)
CODE_TINY = 2.0**-30

MESH = pl.DeviceIdType.MESH
PAIR_SLOTS = (6, 7, 9, 10, 12, 13, 15, 17, 18)
UNITS = 28 - len(PAIR_SLOTS)
LAGS = (2, 4, 7, 10, 13, 17)
ORDER = (3, 1, 2, 0, 4, 5, 6)
DRAIN_LAG = 1
LATE = 1
AHEAD = 2
EARLY = 3


def encode(v):
    size = jnp.maximum(jnp.abs(v), CODE_TINY)
    level = jnp.log2(size) * CODE_STEPS + (CODE_LOW * CODE_STEPS + 0.5)
    return jnp.where(v < 0.0, -level, level).astype(jnp.int32).astype(jnp.int16)


def decode(q):
    level = q.astype(jnp.int32).astype(jnp.float32)
    sign = jnp.clip(level, -1.0, 1.0)
    return sign * jnp.exp2(jnp.abs(level) * (1.0 / CODE_STEPS) - CODE_LOW)


def fold(v):
    half = v.shape[1] // 2
    return jnp.concatenate([v[:, :half], v[:, half:]], axis=0)


def unfold(v):
    half = v.shape[0] // 2
    return jnp.concatenate([v[:half], v[half:]], axis=1)


def kernel(
    mate_bit,
    pair_slots,
    units,
    x_ref,
    g_ref,
    params_ref,
    moment_ref,
    new_params_ref,
    new_moment_ref,
    new_params,
    new_moment,
    x_own,
    x_near,
    xt_own,
    xt_near,
    g_own,
    g_near,
    p_own,
    m_own,
    part,
    ring_out,
    ring_in,
    total,
    fin_out,
    fin_in,
    cross_in,
    mate_out,
    mate_in,
    x_sem,
    g_sem,
    pm_sem,
    near_send,
    near_recv,
    ring_send,
    ring_recv,
    fin_send,
    fin_recv,
    cross_send,
    cross_recv,
    mate_send,
    mate_recv,
    out_sem,
):
    n_pair = len(pair_slots)
    n_flat = units - n_pair
    group = lax.axis_index("group")
    index = lax.axis_index("fsdp")
    z = index % NZ_RING
    side = index // NZ_RING
    near = (group, (1 - side) * NZ_RING + z)
    low = group // 2**mate_bit % 2
    mate = (group + (1 - 2 * low) * 2**mate_bit, index)
    cross = (mate[0], near[1])

    def along(step):
        return (group, side * NZ_RING + (z + step + NZ_RING) % NZ_RING)

    def pair_number(u):
        return sum((u > t).astype(jnp.int32) for t in pair_slots)

    def is_pair(u):
        return sum((u == t).astype(jnp.int32) for t in pair_slots) == 1

    def flat_col(u):
        return pl.multiple_of((u - pair_number(u)) * C, C)

    def pair_col(which, j):
        return pl.multiple_of((n_flat + which * n_pair + j) * C, C)

    def load_g(u, col):
        return pltpu.make_async_copy(
            g_ref.at[:, pl.ds(col, C)], g_own.at[u], g_sem.at[u]
        )

    def own_col(u):
        pair = is_pair(u).astype(jnp.int32)
        j = pair_number(u)
        return pl.multiple_of(
            pair * (n_flat + side * n_pair + j) * C + (1 - pair) * (u - j) * C, C
        )

    barrier = pltpu.get_barrier_semaphore()
    for device in (along(1), along(-1), near, mate, cross):
        pl.semaphore_signal(barrier, inc=1, device_id=device, device_id_type=MESH)

    load_x = pltpu.make_async_copy(x_ref, x_own, x_sem)
    load_x.start()

    @pl.loop(0, units)
    def _(u):
        load_g(u, own_col(u)).start()

    load_p = pltpu.make_async_copy(params_ref.at[0], p_own, pm_sem.at[0])
    load_m = pltpu.make_async_copy(moment_ref.at[0], m_own, pm_sem.at[1])
    load_p.start()
    load_m.start()

    send_x = pltpu.make_async_remote_copy(
        src_ref=x_ref,
        dst_ref=x_near,
        send_sem=near_send.at[n_pair],
        recv_sem=near_recv.at[n_pair],
        device_id=near,
        device_id_type=MESH,
    )

    def send_g(j):
        return pltpu.make_async_remote_copy(
            src_ref=g_ref.at[:, pl.ds(pair_col(1 - side, j), C)],
            dst_ref=g_near.at[j],
            send_sem=near_send.at[j],
            recv_sem=near_recv.at[j],
            device_id=near,
            device_id_type=MESH,
        )

    def ring(u, k, step):
        return pltpu.make_async_remote_copy(
            src_ref=ring_out.at[u, k],
            dst_ref=ring_in.at[u, k],
            send_sem=ring_send.at[u, k],
            recv_sem=ring_recv.at[u, k],
            device_id=along(step),
            device_id_type=MESH,
        )

    def own_rows(u, where):
        first = pl.multiple_of(where * ROWS, 8)
        second = pl.multiple_of(NZ_RING * ROWS + where * ROWS, 8)
        return jnp.concatenate(
            [part[u, pl.ds(first, ROWS), :], part[u, pl.ds(second, ROWS), :]], axis=0
        )

    def turn(u):
        return 1 - 2 * (u % 2)

    def place(u, distance):
        return (z + turn(u) * distance + NZ_RING) % NZ_RING

    def form_flat(u):
        load_g(u, own_col(u)).wait()
        part[u] = jnp.dot(xt_own[...], g_own[u], preferred_element_type=jnp.float32)

    def form_pair(u):
        j = pair_number(u)
        load_g(u, own_col(u)).wait()

        @pl.when(j == 0)
        def _():
            send_x.wait_recv()
            xt_near[...] = x_near[...].astype(jnp.float32).T.astype(jnp.bfloat16)

        send_g(j).wait_recv()

        @pl.when(j + AHEAD < n_pair)
        def _():
            send_g(j + AHEAD).start()

        part[u] = jnp.dot(
            xt_own[...], g_own[u], preferred_element_type=jnp.float32
        ) + jnp.dot(xt_near[...], g_near[j], preferred_element_type=jnp.float32)

    def first_codes(u):
        ring_out[u, 0] = encode(own_rows(u, place(u, 4)))
        ring_out[u, 4] = encode(own_rows(u, place(u, -3)))

    def launch(u):
        ring(u, 0, turn(u)).start()
        ring(u, 4, -turn(u)).start()

    def start(u):
        @pl.when(u >= EARLY)
        def _():
            pair = is_pair(u)
            pl.when(jnp.logical_not(pair))(lambda: form_flat(u))
            pl.when(pair)(lambda: form_pair(u))
            ring_out[u, 0] = encode(own_rows(u, place(u, 4)))
            ring(u, 0, turn(u)).start()
            ring_out[u, 4] = encode(own_rows(u, place(u, -3)))
            ring(u, 4, -turn(u)).start()

    def hop(h, u):
        ring(u, h - 1, turn(u)).wait_recv()
        ring_out[u, h] = encode(decode(ring_in[u, h - 1]) + own_rows(u, place(u, 4 - h)))
        ring(u, h, turn(u)).start()
        if h < 3:
            ring(u, h + 3, -turn(u)).wait_recv()
            ring_out[u, h + 4] = encode(
                decode(ring_in[u, h + 3]) + own_rows(u, place(u, h - 3))
            )
            ring(u, h + 4, -turn(u)).start()

    def fin(u):
        return pltpu.make_async_remote_copy(
            src_ref=fin_out.at[u],
            dst_ref=fin_in.at[u],
            send_sem=fin_send.at[u],
            recv_sem=fin_recv.at[u],
            device_id=near,
            device_id_type=MESH,
        )

    def finish(u):
        ring(u, 6, -turn(u)).wait_recv()
        ring(u, 3, turn(u)).wait_recv()
        total[u] = decode(ring_in[u, 3]) + decode(ring_in[u, 6]) + own_rows(u, z)
        other = total[u, pl.ds(pl.multiple_of((1 - side) * ROWS, 8), ROWS), :]
        fin_out[u] = encode(fold(other))
        fin(u).start()

        @pl.when(u >= units - LATE)
        def _():
            crossing(u).start()
            pair = is_pair(u)
            j = pair_number(u)
            own_sum = total[u, pl.ds(pl.multiple_of(side * ROWS, 8), ROWS), :]

            @pl.when(jnp.logical_not(pair))
            def _():
                half = half_of(flat_col(u), own_sum)
                mate_out[u, :, : C // 2] = encode(fold(half))
                mate_flat(u).start()

            @pl.when(pair)
            def _():
                own_half = half_of(pair_col(side, j), own_sum)
                near_half = half_of(pair_col(1 - side, j), jnp.zeros_like(own_sum))
                mate_out[u] = encode(jnp.concatenate([own_half, near_half], axis=0))
                mate_pair(u).start()


    def crossing(u):
        return pltpu.make_async_remote_copy(
            src_ref=fin_out.at[u],
            dst_ref=cross_in.at[u - (units - LATE)],
            send_sem=cross_send.at[u - (units - LATE)],
            recv_sem=cross_recv.at[u - (units - LATE)],
            device_id=cross,
            device_id_type=MESH,
        )

    def mate_flat(u):
        return pltpu.make_async_remote_copy(
            src_ref=mate_out.at[u, :, pl.ds(0, C // 2)],
            dst_ref=mate_in.at[u, :, pl.ds(0, C // 2)],
            send_sem=mate_send.at[u],
            recv_sem=mate_recv.at[u],
            device_id=mate,
            device_id_type=MESH,
        )

    def mate_pair(u):
        return pltpu.make_async_remote_copy(
            src_ref=mate_out.at[u],
            dst_ref=mate_in.at[u],
            send_sem=mate_send.at[u],
            recv_sem=mate_recv.at[u],
            device_id=mate,
            device_id_type=MESH,
        )

    def out_moment(u, which, col):
        columns = pl.ds(col, C)
        return pltpu.make_async_copy(
            new_moment.at[:, columns],
            new_moment_ref.at[0, :, columns],
            out_sem.at[u, which],
        )

    def out_params(u, which, col):
        columns = pl.ds(col, C)
        return pltpu.make_async_copy(
            new_params.at[:, columns],
            new_params_ref.at[0, :, columns],
            out_sem.at[u, 2 + which],
        )

    def half_of(col, grad):
        columns = pl.ds(col, C)
        moved = MOMENTUM * m_own[:, columns] + grad
        return p_own[:, columns] - RATE * (grad + MOMENTUM * moved)

    def step(u, which, col, grad):
        columns = pl.ds(col, C)
        moved = MOMENTUM * m_own[:, columns] + grad
        half = p_own[:, columns] - RATE * (grad + MOMENTUM * moved)
        new_moment[:, columns] = moved
        new_params[:, columns] = half
        out_moment(u, which, col).start()
        return half

    def mix(u, which, col, got):
        columns = pl.ds(col, C)
        new_params[:, columns] = 0.5 * (new_params[:, columns] + got)
        out_params(u, which, col).start()

    def update(u):
        @pl.when(u == 0)
        def _():
            load_p.wait()
            load_m.wait()

        fin(u).wait_recv()
        near_sum = unfold(decode(fin_in[u]))
        own_sum = total[u, pl.ds(pl.multiple_of(side * ROWS, 8), ROWS), :]
        pair = is_pair(u)
        j = pair_number(u)
        late = u >= units - LATE
        soon = jnp.logical_not(late)

        @pl.when(late)
        def _():
            crossing(u).wait_recv()
            far = (RATE * (1.0 + MOMENTUM)) * unfold(
                decode(cross_in[u - (units - LATE)])
            )

            @pl.when(jnp.logical_not(pair))
            def _():
                col = flat_col(u)
                step(u, 0, col, own_sum + near_sum)
                mate_flat(u).wait_recv()
                mix(u, 0, col, unfold(decode(mate_in[u, :, : C // 2])) - far)

            @pl.when(pair)
            def _():
                step(u, 0, pair_col(side, j), own_sum)
                step(u, 1, pair_col(1 - side, j), near_sum)
                mate_pair(u).wait_recv()
                got = decode(mate_in[u])
                mix(u, 0, pair_col(side, j), got[:ROWS])
                mix(u, 1, pair_col(1 - side, j), got[ROWS:] - far)

        @pl.when(jnp.logical_and(soon, jnp.logical_not(pair)))
        def _():
            half = step(u, 0, flat_col(u), own_sum + near_sum)
            mate_out[u, :, : C // 2] = encode(fold(half))
            mate_flat(u).start()

        @pl.when(jnp.logical_and(soon, pair))
        def _():
            own_half = step(u, 0, pair_col(side, j), own_sum)
            near_half = step(u, 1, pair_col(1 - side, j), near_sum)
            mate_out[u] = encode(jnp.concatenate([own_half, near_half], axis=0))
            mate_pair(u).start()

    def average(u):
        pair = is_pair(u)
        j = pair_number(u)

        soon = u < units - LATE

        @pl.when(jnp.logical_and(soon, jnp.logical_not(pair)))
        def _():
            mate_flat(u).wait_recv()
            mix(u, 0, flat_col(u), unfold(decode(mate_in[u, :, : C // 2])))

        @pl.when(jnp.logical_and(soon, pair))
        def _():
            mate_pair(u).wait_recv()
            got = decode(mate_in[u])
            mix(u, 0, pair_col(side, j), got[:ROWS])
            mix(u, 1, pair_col(1 - side, j), got[ROWS:])

    def drain(u):
        for k in range(4):
            ring(u, k, 1).wait_send()
        for k in range(4, 7):
            ring(u, k, -1).wait_send()
        fin(u).wait_send()

        @pl.when(u >= units - LATE)
        def _():
            crossing(u).wait_send()

        pair = is_pair(u)
        j = pair_number(u)

        @pl.when(pair)
        def _():
            send_g(j).wait_send()
            mate_pair(u).wait_send()
            for which, col in ((0, pair_col(side, j)), (1, pair_col(1 - side, j))):
                out_moment(u, which, col).wait()
                out_params(u, which, col).wait()

        @pl.when(jnp.logical_not(pair))
        def _():
            mate_flat(u).wait_send()
            out_moment(u, 0, flat_col(u)).wait()
            out_params(u, 0, flat_col(u)).wait()

    load_x.wait()
    xt_own[...] = x_own[...].astype(jnp.float32).T.astype(jnp.bfloat16)

    @pl.loop(0, EARLY)
    def _(u):
        form_flat(u)
        first_codes(u)

    pl.semaphore_wait(barrier, 5)
    send_x.start()

    @pl.loop(0, EARLY)
    def _(u):
        launch(u)

    for j in range(AHEAD):
        send_g(j).start()

    actions = (start, partial(hop, 1), partial(hop, 2), partial(hop, 3))
    actions += (finish, update, average)
    lags = (0, *LAGS)
    last = lags[-1]

    @pl.loop(0, units + last + DRAIN_LAG)
    def _(s):
        for k in ORDER:
            u = s - lags[k]
            pl.when(jnp.logical_and(u >= 0, u < units))(partial(actions[k], u))
        u = s - last - DRAIN_LAG
        pl.when(u >= 0)(partial(drain, u))

    send_x.wait_send()


def run(mate_bit, pair_slots, units, activations, cotangent, params, moment):
    n_pair = len(pair_slots)
    any_ref = pl.BlockSpec(memory_space=pl.ANY)
    dma = pltpu.SemaphoreType.DMA
    bf16, f32, i16 = jnp.bfloat16, jnp.float32, jnp.int16
    out = jax.ShapeDtypeStruct((1, ROWS, HID), f32)
    return pl.pallas_call(
        partial(kernel, mate_bit, pair_slots, units),
        out_shape=(out, out),
        in_specs=[any_ref] * 4,
        out_specs=(any_ref, any_ref),
        scratch_shapes=[
            pltpu.VMEM((ROWS, HID), f32),
            pltpu.VMEM((ROWS, HID), f32),
            pltpu.VMEM((TOK, WROWS), bf16),
            pltpu.VMEM((TOK, WROWS), bf16),
            pltpu.VMEM((WROWS, TOK), bf16),
            pltpu.VMEM((WROWS, TOK), bf16),
            pltpu.VMEM((units, TOK, C), bf16),
            pltpu.VMEM((n_pair, TOK, C), bf16),
            pltpu.VMEM((ROWS, HID), f32),
            pltpu.VMEM((ROWS, HID), f32),
            pltpu.VMEM((units, WROWS, C), f32),
            pltpu.VMEM((units, 7, 2 * ROWS, C), i16),
            pltpu.VMEM((units, 7, 2 * ROWS, C), i16),
            pltpu.VMEM((units, 2 * ROWS, C), f32),
            pltpu.VMEM((units, 2 * ROWS, C // 2), i16),
            pltpu.VMEM((units, 2 * ROWS, C // 2), i16),
            pltpu.VMEM((LATE, 2 * ROWS, C // 2), i16),
            pltpu.VMEM((units, 2 * ROWS, C), i16),
            pltpu.VMEM((units, 2 * ROWS, C), i16),
            dma,
            dma((units,)),
            dma((2,)),
            dma((n_pair + 1,)),
            dma((n_pair + 1,)),
            dma((units, 7)),
            dma((units, 7)),
            dma((units,)),
            dma((units,)),
            dma((LATE,)),
            dma((LATE,)),
            dma((units,)),
            dma((units,)),
            dma((units, 4)),
        ],
        compiler_params=pltpu.CompilerParams(
            collective_id=mate_bit, has_side_effects=True, vmem_limit_bytes=50 << 20
        ),
        cost_estimate=pl.CostEstimate(
            flops=2 * TOK * WROWS * HID, bytes_accessed=13 << 20, transcendentals=0
        ),
    )(activations, cotangent, params, moment)


def on_device(activations, cotangent, params, moment, step_index):
    bits = lax.axis_size("group").bit_length() - 1
    branches = [partial(run, bit, PAIR_SLOTS, UNITS) for bit in range(bits)]
    return lax.switch(
        step_index % bits, branches, activations, cotangent, params, moment
    )


def solution(mesh):
    in_specs = (
        P(("group", "fsdp"), None),
        P(("group", "fsdp"), None),
        P("group", "fsdp", None),
        P("group", "fsdp", None),
        P(),
    )
    out_specs = (P("group", "fsdp", None), P("group", "fsdp", None))
    return jax.shard_map(
        on_device, mesh=mesh, in_specs=in_specs, out_specs=out_specs, check_vma=False
    )
```
